256 devices in a mesh: ctx: 16 (over z, core), ulys: 16 (over y, x).
Axes of the slice: x: 4, y: 4, z: 8, core: 2. Of those that a mesh axis runs over, the one named last changes fastest.
Arguments:
- query_rows: bfloat16 [32768, 4096], P(('ctx', 'ulys')), may hold values from -8 to 8
- key_rows: bfloat16 [32768, 512], P(('ctx', 'ulys')), may hold values from -8 to 8
- value_rows: bfloat16 [32768, 512], P(('ctx', 'ulys')), may hold values from -6 to 6
- column_blocks: int32 [32, 8], replicated, may hold values from 0 to 511, as said below
- column_count: int32 [32], replicated, may hold values from 1 to 8, as said below
- slash_offsets: int32 [32, 24], replicated, may hold values from 1 to 504, as said below
- slash_count: int32 [32], replicated, may hold values from 1 to 24, as said below
Outputs:
- attended: bfloat16 [32768, 4096], P(('ctx', 'ulys'))
The draws below stay inside these ranges and needn't reach their ends.
Inputs may be any that keep to these rules, and one draw needn't show every extreme that they name: `column_blocks`: within a head the entries increase; the a-th lies among blocks a * (512 // 8) to (a + 1) * (512 // 8) - 1, with 512 // 8 = 64. `column_count`: some head uses all 8. `slash_offsets`: within a head the entries increase; the s-th lies among offsets 1 + s * ((512 - 1) // 24) to (s + 1) * ((512 - 1) // 24). `slash_count`: some head uses all 24.
All inputs are finite; a program needn't handle non-finite values.
Results may differ from the reference program's by a relative error of at most 0.0049.
Values may be sent and summed in bfloat16 or wider, within the bound.
No kernel may reach another device: no remote copies, remote signals or barrier semaphores. Data moves between devices by JAX's collectives and lax.ppermute only.
A program may use at most 128 MiB of HBM per device.

```python
import math
import jax
import jax.numpy as jnp
from jax import lax

H = 32
KVH = 4
DH = 128
BLK = 64
NV = 8
NS = 24
SEQ = 32768
NB = 512


def draw_query_rows(key, part):
    key = jax.random.fold_in(key, 3)
    drawn = jnp.clip(jax.random.normal(key, (SEQ, H * DH)), -8.0, 8.0)
    return drawn.astype(jnp.bfloat16)


def draw_key_rows(key, part):
    key = jax.random.fold_in(key, 4)
    drawn = jnp.clip(jax.random.normal(key, (SEQ, KVH * DH)), -8.0, 8.0)
    return drawn.astype(jnp.bfloat16)


def runs_with_ends(key, rows, width, run_length, first):
    starts = first + jnp.arange(width, dtype=jnp.int32)[None, :] * run_length
    drawn = jax.random.randint(key, (rows, width), 0, run_length)
    chosen = jax.random.randint(jax.random.fold_in(key, 2), (), 0, rows)
    columns = jnp.arange(width, dtype=jnp.int32)[None, :]
    is_chosen = (jnp.arange(rows, dtype=jnp.int32) == chosen)[:, None]
    drawn = jnp.where(is_chosen & (columns == 0), 0, drawn)
    drawn = jnp.where(is_chosen & (columns == width - 1), run_length - 1, drawn)
    return (starts + drawn).astype(jnp.int32)


def draw_column_blocks(key, part):
    key = jax.random.fold_in(key, 5)
    return runs_with_ends(key, H, NV, NB // NV, 0)


def draw_slash_offsets(key, part):
    key = jax.random.fold_in(key, 7)
    return runs_with_ends(key, H, NS, (NB - 1) // NS, 1)


def counts_with_top(key, most):
    counts = jax.random.randint(key, (H,), 1, most + 1)
    chosen = jax.random.randint(jax.random.fold_in(key, 1), (), 0, H)
    return jnp.where(jnp.arange(H) == chosen, most, counts).astype(jnp.int32)


def draw_column_count(key, part):
    key = jax.random.fold_in(key, 9)
    return counts_with_top(key, NV)


def draw_slash_count(key, part):
    key = jax.random.fold_in(key, 11)
    return counts_with_top(key, NS)


def block_scale(stream_key, extent, cuts, low, high):
    factor_of = 1.0
    for position, parts in cuts:
        steps = jax.random.uniform(jax.random.fold_in(jax.random.fold_in(stream_key, 6), position), (parts,), jnp.float32, low / len(cuts), high / len(cuts))
        factor_of = factor_of * jnp.repeat(jnp.exp(steps), extent[position] // parts).reshape((-1,) + (1,) * (len(extent) - 1 - position))
    return factor_of


def scatter_about(stream_key, extent, scale, reach, split=(), kind=jnp.bfloat16):
    factor_of = block_scale(stream_key, extent, split, -0.22, 0.18) if split else 1.0
    values = jax.random.normal(stream_key, extent, jnp.float32) * scale * factor_of
    return jnp.minimum(jnp.maximum(values, -reach), reach).astype(kind)


def setup_inputs(seed: int = 0) -> dict:
    streams_of = jax.random.split(jax.random.key(seed), 8)
    return {
        "query_rows": draw_query_rows(jax.random.fold_in(streams_of[7], 71), 0),
        "key_rows": draw_key_rows(jax.random.fold_in(streams_of[7], 71), 0),
        "value_rows": scatter_about(streams_of[2], (SEQ, KVH * DH), 1.0, 6.0, ((0, 256),)),
        "column_blocks": draw_column_blocks(jax.random.fold_in(streams_of[7], 71), 0),
        "column_count": draw_column_count(jax.random.fold_in(streams_of[7], 71), 0),
        "slash_offsets": draw_slash_offsets(jax.random.fold_in(streams_of[7], 71), 0),
        "slash_count": draw_slash_count(jax.random.fold_in(streams_of[7], 71), 0),
    }


def block_lists(query_block, column_row, column_live, slash_row, slash_live):
    own_block = query_block[:, None]
    upto_column = jnp.arange(NV, dtype=jnp.int32) < column_live
    column_ok = upto_column[None, :] & (column_row[None, :] < own_block)
    slash_blocks = own_block - slash_row[None, :]
    already = jnp.any((column_row[None, None, :] == slash_blocks[:, :, None]) & upto_column[None, None, :], axis=2)
    upto_slash = jnp.arange(NS, dtype=jnp.int32) < slash_live
    slash_ok = upto_slash[None, :] & (slash_blocks >= 0) & jnp.logical_not(already)
    column_wide = jnp.broadcast_to(column_row[None, :], (query_block.shape[0], NV))
    blocks = jnp.concatenate([own_block, column_wide, slash_blocks], axis=1).astype(jnp.int32)
    usable = jnp.concatenate([jnp.ones(own_block.shape, dtype=bool), column_ok, slash_ok], axis=1)
    return (blocks, usable)

def reference(query_rows, key_rows, value_rows, column_blocks, column_count, slash_offsets, slash_count):
    per_group = H // KVH
    span_blocks = math.gcd(NB, 8)
    rescale_factor = 1.0 / math.sqrt(DH)
    causal = jnp.arange(BLK)[None, :] <= jnp.arange(BLK)[:, None]
    is_local = jnp.arange(1 + NV + NS) == 0

    def one_head(head_index):
        kv_head = head_index // per_group
        q_all = lax.dynamic_slice_in_dim(query_rows, head_index * DH, DH, 1).reshape(NB, BLK, DH)
        k_all = lax.dynamic_slice_in_dim(key_rows, kv_head * DH, DH, 1).reshape(NB, BLK, DH)
        v_all = lax.dynamic_slice_in_dim(value_rows, kv_head * DH, DH, 1).reshape(NB, BLK, DH)

        def one_span(span_start):
            query_block = span_start + jnp.arange(span_blocks, dtype=jnp.int32)
            blocks, usable = block_lists(query_block, column_blocks[head_index], column_count[head_index], slash_offsets[head_index], slash_count[head_index])
            clipped = jnp.clip(blocks, 0, NB - 1).astype(jnp.int32)
            query_slice = lax.dynamic_slice_in_dim(q_all, span_start, span_blocks, 0).astype(jnp.float32)
            key_slice = k_all[clipped].astype(jnp.float32)
            value_slice = v_all[clipped].astype(jnp.float32)
            logit_scores = jnp.einsum('zyu,zwiu->zywi', query_slice, key_slice) * rescale_factor
            visible = usable[:, None, :, None] & (jnp.logical_not(is_local)[None, None, :, None] | causal[None, :, None, :])
            logit_scores = jnp.where(visible, logit_scores, jnp.float32(-1e+30))
            row_top = lax.optimization_barrier(jnp.max(logit_scores, axis=(2, 3), keepdims=True))
            exponent = jnp.where(visible, jnp.exp(logit_scores - row_top), jnp.float32(0.0))
            denominator = lax.optimization_barrier(jnp.sum(exponent, axis=(2, 3)))
            softmax_weights = lax.optimization_barrier(exponent.astype(jnp.bfloat16)).astype(jnp.float32)
            weight_totals = jnp.einsum('slhe,sher->slr', softmax_weights, value_slice)
            return (weight_totals / denominator[:, :, None]).astype(jnp.bfloat16)
        span_starts = jnp.arange(0, NB, span_blocks, dtype=jnp.int32)
        return lax.map(one_span, span_starts).reshape(SEQ, DH)
    per_head = lax.map(one_head, jnp.arange(H, dtype=jnp.int32))
    return jnp.transpose(per_head, (1, 0, 2)).reshape(SEQ, H * DH)
```

```python
import math

import jax
import jax.numpy as jnp
from jax import lax
from jax.experimental import pallas as pl
from jax.experimental.pallas import tpu as pltpu
from jax.sharding import Mesh, PartitionSpec as P

H = 32
KVH = 4
DH = 128
BLK = 64
NV = 8
NS = 24
SEQ = 32768

QB = 8
HG = H // KVH
CB = 4
CHUNKS = -(-(1 + NV + NS) // CB)
LMAX = CHUNKS * CB
SKEW = 4
C2 = math.log2(math.e) / math.sqrt(DH)
NEG = -1e30
NT = (((1,), (1,)), ((), ()))


def attend_kernel(
    lists, counts, q_ref, kv_hbm, o_ref, k_s, v_s, top_s, sum_s, acc_s, score_s, sem
):
    copy_k = pltpu.make_async_copy(kv_hbm.at[:, pl.ds(0, DH)], k_s, sem.at[0])
    copy_v = pltpu.make_async_copy(kv_hbm.at[:, pl.ds(DH, DH)], v_s, sem.at[1])
    copy_k.start()
    copy_v.start()
    copy_k.wait()
    copy_v.wait()
    lane = lax.broadcasted_iota(jnp.int32, (BLK, CB * BLK), 1)
    row = lax.broadcasted_iota(jnp.int32, (BLK, CB * BLK), 0)
    lane_row = lax.broadcasted_iota(jnp.int32, (1, CB * BLK), 1)

    def rows(i):
        return slice(i * BLK, (i + 1) * BLK)

    def head(h, _):
        columns = pl.ds(pl.multiple_of(h * DH, DH), DH)

        def gather(ref, i, c):
            base = (h * QB + i) * LMAX + c * CB
            return jnp.concatenate(
                [
                    ref[pl.ds(pl.multiple_of(lists[base + j] * BLK, BLK), BLK), :]
                    for j in range(CB)
                ],
                axis=0,
            )

        def scores(i, c):
            return lax.dot_general(
                q_ref[rows(i), columns],
                gather(k_s, i, c),
                NT,
                preferred_element_type=jnp.float32,
            )

        def weighted(i, c, p):
            return jnp.dot(p, gather(v_s, i, c), preferred_element_type=jnp.float32)

        def first_weights(i, s):
            live = counts[HG + h * QB + i]
            s = jnp.where((lane < live * BLK) & ((lane >= BLK) | (lane <= row)), s, NEG)
            top = jnp.max(jnp.maximum(s[:, :128], s[:, 128:]), axis=1, keepdims=True)
            shift = top * C2
            parts = [jnp.exp2(s[:, t * 128 : (t + 1) * 128] * C2 - shift) for t in range(2)]
            top_s[rows(i), :] = jnp.broadcast_to(top, (BLK, DH))
            sum_s[rows(i), :] = parts[0] + parts[1]
            return jnp.concatenate([x.astype(jnp.bfloat16) for x in parts], axis=1)

        def next_weights(i, c, s):
            live = counts[HG + h * QB + i]
            s = s + jnp.where(lane_row < (live - c * CB) * BLK, 0.0, NEG)
            old = top_s[rows(i), :]
            top = jnp.maximum(
                old, jnp.max(jnp.maximum(s[:, :128], s[:, 128:]), axis=1, keepdims=True)
            )
            shrink = jnp.exp2((old - top) * C2)
            shift = top * C2
            parts = [jnp.exp2(s[:, t * 128 : (t + 1) * 128] * C2 - shift) for t in range(2)]
            top_s[rows(i), :] = top
            sum_s[rows(i), :] = sum_s[rows(i), :] * shrink + (parts[0] + parts[1])
            return jnp.concatenate([x.astype(jnp.bfloat16) for x in parts], axis=1), shrink

        opening = [scores(i, 0) for i in range(QB)]
        for i in range(QB):
            score_s[rows(i), :] = scores(i, 1)
        weights = [first_weights(i, s) for i, s in enumerate(opening)]
        for i, p in enumerate(weights):
            acc_s[rows(i), :] = weighted(i, 0, p)

        def chunk(c, _):
            ahead = jnp.minimum(c + 1, CHUNKS - 1)
            held = {}
            for t in range(QB + SKEW):
                if t < QB:
                    s = score_s[rows(t), :]
                    score_s[rows(t), :] = scores(t, ahead)
                    held[t] = next_weights(t, c, s)
                i = t - SKEW
                if i >= 0:
                    p, shrink = held.pop(i)
                    acc_s[rows(i), :] = acc_s[rows(i), :] * shrink + weighted(i, c, p)
            return 0

        lax.fori_loop(1, counts[h], chunk, 0)
        for i in range(QB):
            total = jnp.sum(sum_s[rows(i), :], axis=1, keepdims=True)
            o_ref[rows(i), columns] = (acc_s[rows(i), :] / total).astype(jnp.bfloat16)
        return 0

    lax.fori_loop(0, HG, head, 0)


def attend(lists, counts, queries, pairs):
    any_space = pl.BlockSpec(memory_space=pl.ANY)
    vmem = pl.BlockSpec(memory_space=pltpu.VMEM)
    smem = pl.BlockSpec(memory_space=pltpu.SMEM)
    return pl.pallas_call(
        attend_kernel,
        out_shape=jax.ShapeDtypeStruct((QB * BLK, HG * DH), jnp.bfloat16),
        in_specs=[smem, smem, vmem, any_space],
        out_specs=vmem,
        scratch_shapes=[pltpu.VMEM((SEQ, DH), jnp.bfloat16)] * 2
        + [pltpu.VMEM((QB * BLK, DH), jnp.float32)] * 3
        + [pltpu.VMEM((QB * BLK, CB * BLK), jnp.float32), pltpu.SemaphoreType.DMA((2,))],
        compiler_params=pltpu.CompilerParams(vmem_limit_bytes=40 * 1024 * 1024),
    )(lists, counts, queries, pairs)


def block_lists(first_block, column_blocks, column_count, slash_offsets, slash_count):
    own = first_block + jnp.arange(QB, dtype=jnp.int32)[None, :, None]
    own = jnp.broadcast_to(own, (HG, QB, 1))
    column = jnp.broadcast_to(column_blocks[:, None, :], (HG, QB, NV))
    column_used = jnp.arange(NV, dtype=jnp.int32) < column_count[:, None, None]
    slash = own - slash_offsets[:, None, :]
    slash_used = jnp.arange(NS, dtype=jnp.int32) < slash_count[:, None, None]
    twice = jnp.any(
        (column[:, :, None, :] == slash[:, :, :, None]) & column_used[:, :, None, :], axis=3
    )
    blocks = jnp.concatenate([own, column, slash], axis=2)
    usable = jnp.concatenate(
        [
            jnp.ones(own.shape, bool),
            column_used & (column < own),
            slash_used & (slash >= 0) & jnp.logical_not(twice),
        ],
        axis=2,
    )
    width = 1 + NV + NS
    earlier = jnp.arange(width)[None, :] < jnp.arange(width)[:, None]
    place = jnp.sum(usable[:, :, None, :] & earlier, axis=3, dtype=jnp.int32)
    live = jnp.sum(usable, axis=2, dtype=jnp.int32)
    slot = jnp.arange(LMAX, dtype=jnp.int32)
    chosen = usable[:, :, None, :] & (place[:, :, None, :] == slot[:, None])
    packed = jnp.sum(jnp.where(chosen, blocks[:, :, None, :], 0), axis=3)
    packed = jnp.where(slot < live[:, :, None], packed, own)
    steps = (jnp.max(live, axis=1) + CB - 1) // CB
    return packed.reshape(-1), jnp.concatenate([steps, live.reshape(-1)])


def per_device(
    query_rows, key_rows, value_rows, column_blocks, column_count, slash_offsets, slash_count
):
    tokens = query_rows.shape[0]
    group = lax.axis_index("x")
    place = (lax.axis_index("z") * 2 + lax.axis_index("core")) * 4 + lax.axis_index("y")
    pairs = jnp.concatenate(
        [key_rows.reshape(tokens, KVH, DH), value_rows.reshape(tokens, KVH, DH)], axis=2
    )
    pairs = lax.all_to_all(pairs, "x", split_axis=1, concat_axis=0, tiled=True)
    pairs = pairs.reshape(QB * BLK, 2 * DH)
    queries = lax.all_to_all(
        query_rows.reshape(tokens, KVH, HG * DH), "x", split_axis=1, concat_axis=0, tiled=True
    ).reshape(QB * BLK, HG * DH)
    all_pairs = lax.all_gather(pairs, ("z", "core", "y"), axis=0, tiled=True)

    def mine(array):
        return lax.dynamic_slice_in_dim(array, group * HG, HG, 0)

    lists, counts = block_lists(
        place * QB, mine(column_blocks), mine(column_count), mine(slash_offsets), mine(slash_count)
    )
    outputs = attend(lists, counts, queries, all_pairs)
    returned = lax.all_to_all(
        outputs.reshape(KVH, tokens, HG * DH), "x", split_axis=0, concat_axis=2, tiled=True
    )
    return returned.reshape(tokens, H * DH)


def solution(mesh):
    fine = Mesh(mesh.devices.reshape(8, 2, 4, 4), ("z", "core", "y", "x"))
    split = P(("z", "core", "y", "x"), None)
    return jax.shard_map(
        per_device,
        mesh=fine,
        in_specs=(split, split, split, P(), P(), P(), P()),
        out_specs=split,
        check_vma=False,
    )
```

```python
import math

import jax
import jax.numpy as jnp
from jax import lax
from jax.experimental import pallas as pl
from jax.experimental.pallas import tpu as pltpu
from jax.sharding import Mesh, PartitionSpec as P

H = 32
KVH = 4
DH = 128
BLK = 64
NV = 8
NS = 24
SEQ = 32768

QB = 8
HG = H // KVH
CB = 4
CHUNKS = -(-(1 + NV + NS) // CB)
LMAX = CHUNKS * CB
SKEW = 4
C2 = math.log2(math.e) / math.sqrt(DH)
NEG = -1e30
NT = (((1,), (1,)), ((), ()))
PIECE = SEQ // 8


def attend_kernel(k_lists, v_lists, counts, q_ref, *refs):
    held, swapped, o_ref = refs[:10], refs[10:20], refs[20]
    k_s, v_s, top_s, sum_s, acc_s, score_s, sem = refs[21:]
    is_first = counts[HG + HG * QB] == 0

    def load(keys, values):
        copies = []
        for p in range(7):
            copies.append((keys[p], k_s.at[pl.ds(p * PIECE, PIECE), :]))
            copies.append((values[p], v_s.at[pl.ds(p * PIECE, PIECE), :]))
        half = PIECE // 2
        copies.append((keys[7], k_s.at[pl.ds(7 * PIECE, half), :]))
        copies.append((keys[8], k_s.at[pl.ds(7 * PIECE + half, half), :]))
        copies.append((values[9], v_s.at[pl.ds(7 * PIECE, PIECE), :]))
        started = [
            pltpu.make_async_copy(source, target, sem.at[n])
            for n, (source, target) in enumerate(copies)
        ]
        for copy in started:
            copy.start()
        for copy in started:
            copy.wait()

    @pl.when(is_first)
    def _():
        load(held, swapped)

    @pl.when(jnp.logical_not(is_first))
    def _():
        load(swapped, held)

    lane = lax.broadcasted_iota(jnp.int32, (BLK, CB * BLK), 1)
    row = lax.broadcasted_iota(jnp.int32, (BLK, CB * BLK), 0)
    lane_row = lax.broadcasted_iota(jnp.int32, (1, CB * BLK), 1)

    def rows(i):
        return slice(i * BLK, (i + 1) * BLK)

    def head(h, _):
        columns = pl.ds(pl.multiple_of(h * DH, DH), DH)

        def gather(ref, lists, i, c):
            base = (h * QB + i) * LMAX + c * CB
            return jnp.concatenate(
                [
                    ref[pl.ds(pl.multiple_of(lists[base + j] * BLK, BLK), BLK), :]
                    for j in range(CB)
                ],
                axis=0,
            )

        def scores(i, c):
            return lax.dot_general(
                q_ref[rows(i), columns],
                gather(k_s, k_lists, i, c),
                NT,
                preferred_element_type=jnp.float32,
            )

        def weighted(i, c, p):
            return jnp.dot(p, gather(v_s, v_lists, i, c), preferred_element_type=jnp.float32)

        def first_weights(i, s):
            live = counts[HG + h * QB + i]
            s = jnp.where((lane < live * BLK) & ((lane >= BLK) | (lane <= row)), s, NEG)
            top = jnp.max(jnp.maximum(s[:, :128], s[:, 128:]), axis=1, keepdims=True)
            shift = top * C2
            parts = [jnp.exp2(s[:, t * 128 : (t + 1) * 128] * C2 - shift) for t in range(2)]
            top_s[rows(i), :] = jnp.broadcast_to(top, (BLK, DH))
            sum_s[rows(i), :] = parts[0] + parts[1]
            return jnp.concatenate([x.astype(jnp.bfloat16) for x in parts], axis=1)

        def next_weights(i, c, s):
            live = counts[HG + h * QB + i]
            s = s + jnp.where(lane_row < (live - c * CB) * BLK, 0.0, NEG)
            old = top_s[rows(i), :]
            top = jnp.maximum(
                old, jnp.max(jnp.maximum(s[:, :128], s[:, 128:]), axis=1, keepdims=True)
            )
            shrink = jnp.exp2((old - top) * C2)
            shift = top * C2
            parts = [jnp.exp2(s[:, t * 128 : (t + 1) * 128] * C2 - shift) for t in range(2)]
            top_s[rows(i), :] = top
            sum_s[rows(i), :] = sum_s[rows(i), :] * shrink + (parts[0] + parts[1])
            return jnp.concatenate([x.astype(jnp.bfloat16) for x in parts], axis=1), shrink

        opening = [scores(i, 0) for i in range(QB)]
        for i in range(QB):
            score_s[rows(i), :] = scores(i, 1)
        weights = [first_weights(i, s) for i, s in enumerate(opening)]
        for i, p in enumerate(weights):
            acc_s[rows(i), :] = weighted(i, 0, p)

        def chunk(c, _):
            ahead = jnp.minimum(c + 1, CHUNKS - 1)
            held = {}
            for t in range(QB + SKEW):
                if t < QB:
                    s = score_s[rows(t), :]
                    score_s[rows(t), :] = scores(t, ahead)
                    held[t] = next_weights(t, c, s)
                i = t - SKEW
                if i >= 0:
                    p, shrink = held.pop(i)
                    acc_s[rows(i), :] = acc_s[rows(i), :] * shrink + weighted(i, c, p)
            return 0

        lax.fori_loop(1, counts[h], chunk, 0)
        for i in range(QB):
            total = jnp.sum(sum_s[rows(i), :], axis=1, keepdims=True)
            o_ref[rows(i), columns] = (acc_s[rows(i), :] / total).astype(jnp.bfloat16)
        return 0

    lax.fori_loop(0, HG, head, 0)


def attend(k_lists, v_lists, counts, queries, held, swapped):
    any_space = pl.BlockSpec(memory_space=pl.ANY)
    vmem = pl.BlockSpec(memory_space=pltpu.VMEM)
    smem = pl.BlockSpec(memory_space=pltpu.SMEM)
    return pl.pallas_call(
        attend_kernel,
        out_shape=jax.ShapeDtypeStruct((QB * BLK, HG * DH), jnp.bfloat16),
        in_specs=[smem] * 3 + [vmem] + [any_space] * 20,
        out_specs=vmem,
        scratch_shapes=[pltpu.VMEM((SEQ, DH), jnp.bfloat16)] * 2
        + [pltpu.VMEM((QB * BLK, DH), jnp.float32)] * 3
        + [pltpu.VMEM((QB * BLK, CB * BLK), jnp.float32), pltpu.SemaphoreType.DMA((17,))],
        compiler_params=pltpu.CompilerParams(vmem_limit_bytes=40 * 1024 * 1024),
    )(k_lists, v_lists, counts, queries, *held, *swapped)


def block_lists(first_block, column_blocks, column_count, slash_offsets, slash_count):
    own = first_block + jnp.arange(QB, dtype=jnp.int32)[None, :, None]
    own = jnp.broadcast_to(own, (HG, QB, 1))
    column = jnp.broadcast_to(column_blocks[:, None, :], (HG, QB, NV))
    column_used = jnp.arange(NV, dtype=jnp.int32) < column_count[:, None, None]
    slash = own - slash_offsets[:, None, :]
    slash_used = jnp.arange(NS, dtype=jnp.int32) < slash_count[:, None, None]
    twice = jnp.any(
        (column[:, :, None, :] == slash[:, :, :, None]) & column_used[:, :, None, :], axis=3
    )
    blocks = jnp.concatenate([own, column, slash], axis=2)
    usable = jnp.concatenate(
        [
            jnp.ones(own.shape, bool),
            column_used & (column < own),
            slash_used & (slash >= 0) & jnp.logical_not(twice),
        ],
        axis=2,
    )
    width = 1 + NV + NS
    earlier = jnp.arange(width)[None, :] < jnp.arange(width)[:, None]
    place = jnp.sum(usable[:, :, None, :] & earlier, axis=3, dtype=jnp.int32)
    live = jnp.sum(usable, axis=2, dtype=jnp.int32)
    slot = jnp.arange(LMAX, dtype=jnp.int32)
    chosen = usable[:, :, None, :] & (place[:, :, None, :] == slot[:, None])
    packed = jnp.sum(jnp.where(chosen, blocks[:, :, None, :], 0), axis=3)
    packed = jnp.where(slot < live[:, :, None], packed, own)
    steps = (jnp.max(live, axis=1) + CB - 1) // CB
    return packed, steps, live


def ring_place(d, size):
    return jnp.where(d < size // 2, 2 * d, 2 * size - 1 - 2 * d)


def piece_places(blocks, z, y):
    dz = ring_place((blocks // 64 - z) % 8, 8)
    dy = (blocks // 8 % 4 - y) % 4
    inner = blocks // 32 % 2 * 8 + blocks % 8
    keys = dz * 64 + ring_place(dy, 4) * 16 + inner
    far = dz // 4
    piece = jnp.where(
        dy == 0,
        7 * far,
        jnp.where(dy == 3, 1 + 2 * far, jnp.where(dy == 1, 2 + 2 * far, 5 + far)),
    )
    values = piece * 64 + dz % 4 * 16 + inner
    return keys, values


def device_index(z, core, y, x):
    return ((z * 2 + core) * 4 + y) * 4 + x


def send(array, first, second):
    pairs = []
    for z in range(8):
        for y in range(4):
            for x in range(4):
                for core, way in enumerate((first, second)):
                    if way is not None:
                        dz, dc, dy = way
                        pairs.append(
                            (
                                device_index(z, core, y, x),
                                device_index((z + dz) % 8, core ^ dc, (y + dy) % 4, x),
                            )
                        )
    return lax.ppermute(array, AXES, pairs)


UP_Z, DOWN_Z, UP_Y, DOWN_Y, OTHER = (1, 0, 0), (-1, 0, 0), (0, 0, 1), (0, 0, -1), (0, 1, 0)
AXES = ("z", "core", "y", "x")


def gather_pairs(own):
    is_first = lax.axis_index("core") == 0
    half = PIECE // 2
    up1 = send(own, UP_Y, UP_Z)
    down1 = send(own, DOWN_Y, DOWN_Z)
    up2 = send(up1, UP_Y, UP_Z)
    near = jnp.concatenate([own, up1, down1, up2])
    down2 = send(down1, None, DOWN_Z)
    up3 = send(up2, None, UP_Z)
    a1 = send(near, UP_Z, UP_Y)
    b1 = send(near, DOWN_Z, DOWN_Y)
    down3 = send(down2, None, DOWN_Z)
    up4 = send(up3, None, UP_Z)
    far = jnp.concatenate([down2, up3, down3, up4])
    a2 = send(jnp.where(is_first, a1, far), UP_Z, UP_Y)
    b2 = send(jnp.where(is_first, b1, far), DOWN_Z, DOWN_Y)
    a3 = send(jnp.where(is_first, a2, a1), UP_Z, UP_Y)
    b3 = send(b2, DOWN_Z, DOWN_Y)
    a4 = send(a3[:half], UP_Z, None)
    b4 = send(b3[half:], DOWN_Z, None)
    held = (near, a1, b1, a2, b2, a3, b3)
    swapped = tuple(send(piece, OTHER, OTHER) for piece in held)
    ends = (send(a4, OTHER, None), send(b4, OTHER, None), send(far, None, OTHER))
    return held + (a4, b4, far), swapped + ends


def per_device(
    query_rows, key_rows, value_rows, column_blocks, column_count, slash_offsets, slash_count
):
    tokens = query_rows.shape[0]
    group = lax.axis_index("x")
    z, core, y = (lax.axis_index(name) for name in ("z", "core", "y"))
    pairs = jnp.concatenate(
        [
            array.reshape(tokens, KVH, DH).transpose(1, 0, 2)
            for array in (key_rows, value_rows)
        ]
    )
    own = lax.all_to_all(pairs, ("core", "x"), split_axis=0, concat_axis=0, tiled=True)
    held, swapped = gather_pairs(own.reshape(8 * tokens, DH))
    queries = lax.all_to_all(
        query_rows.reshape(tokens, KVH, HG * DH), "x", split_axis=1, concat_axis=0, tiled=True
    ).reshape(QB * BLK, HG * DH)

    def mine(array):
        return lax.dynamic_slice_in_dim(array, group * HG, HG, 0)

    blocks, steps, live = block_lists(
        ((z * 2 + core) * 4 + y) * QB,
        mine(column_blocks),
        mine(column_count),
        mine(slash_offsets),
        mine(slash_count),
    )
    k_lists, v_lists = piece_places(blocks, z, y)
    counts = jnp.concatenate([steps, live.reshape(-1), core[None]])
    outputs = attend(k_lists.reshape(-1), v_lists.reshape(-1), counts, queries, held, swapped)
    returned = lax.all_to_all(
        outputs.reshape(KVH, tokens, HG * DH), "x", split_axis=0, concat_axis=2, tiled=True
    )
    return returned.reshape(tokens, H * DH)


def solution(mesh):
    fine = Mesh(mesh.devices.reshape(8, 2, 4, 4), ("z", "core", "y", "x"))
    split = P(("z", "core", "y", "x"), None)
    return jax.shard_map(
        per_device,
        mesh=fine,
        in_specs=(split, split, split, P(), P(), P(), P()),
        out_specs=split,
        check_vma=False,
    )
```

```python
import math

import jax
import jax.numpy as jnp
from jax import lax
from jax.experimental import pallas as pl
from jax.experimental.pallas import tpu as pltpu
from jax.sharding import Mesh, PartitionSpec as P

H = 32
KVH = 4
DH = 128
BLK = 64
NV = 8
NS = 24
SEQ = 32768

QB = 8
HG = H // KVH
CB = 4
CHUNKS = -(-(1 + NV + NS) // CB)
LMAX = CHUNKS * CB
SKEW = 4
C2 = math.log2(math.e) / math.sqrt(DH)
NEG = -1e30
NT = (((1,), (1,)), ((), ()))
PIECE = SEQ // 8


def attend_kernel(k_lists, v_lists, counts, *refs):
    q_refs, held, swapped, o_refs = refs[:4], refs[4:12], refs[12:20], refs[20:24]
    k_s, v_s, top_s, sum_s, acc_s, score_s, sem = refs[24:]
    is_first = counts[HG + HG * QB] == 0

    def copies(source, target, first_sem):
        return [
            pltpu.make_async_copy(
                piece, target.at[pl.ds(p * PIECE, PIECE), :], sem.at[first_sem + p]
            )
            for p, piece in enumerate(source)
        ]

    @pl.when(is_first)
    def _():
        for copy in copies(held, k_s, 0) + copies(swapped, v_s, 8):
            copy.start()

    @pl.when(jnp.logical_not(is_first))
    def _():
        for copy in copies(swapped, k_s, 0) + copies(held, v_s, 8):
            copy.start()

    for copy in copies(held, k_s, 0):
        copy.wait()
    lane = lax.broadcasted_iota(jnp.int32, (BLK, CB * BLK), 1)
    row = lax.broadcasted_iota(jnp.int32, (BLK, CB * BLK), 0)
    lane_row = lax.broadcasted_iota(jnp.int32, (1, CB * BLK), 1)

    def rows(i):
        return slice(i * BLK, (i + 1) * BLK)

    def head(h, _):
        columns = pl.ds(pl.multiple_of(h * DH, DH), DH)

        def gather(ref, lists, i, c):
            base = c * (CB * HG * QB) + (h * QB + i)
            return jnp.concatenate(
                [
                    ref[pl.ds(pl.multiple_of(lists[base + j * (HG * QB)] * BLK, BLK), BLK), :]
                    for j in range(CB)
                ],
                axis=0,
            )

        def scores(i, c):
            return lax.dot_general(
                q_refs[i // 2][rows(i % 2), columns],
                gather(k_s, k_lists, i, c),
                NT,
                preferred_element_type=jnp.float32,
            )

        def weighted(i, c, p):
            return jnp.dot(p, gather(v_s, v_lists, i, c), preferred_element_type=jnp.float32)

        def first_weights(i, s):
            live = counts[HG + h * QB + i]
            s = jnp.where((lane < live * BLK) & ((lane >= BLK) | (lane <= row)), s, NEG)
            top = jnp.max(jnp.maximum(s[:, :128], s[:, 128:]), axis=1, keepdims=True)
            shift = top * C2
            parts = [jnp.exp2(s[:, t * 128 : (t + 1) * 128] * C2 - shift) for t in range(2)]
            top_s[rows(i), :] = jnp.broadcast_to(top, (BLK, DH))
            sum_s[rows(i), :] = parts[0] + parts[1]
            return jnp.concatenate([x.astype(jnp.bfloat16) for x in parts], axis=1)

        def next_weights(i, c, s):
            live = counts[HG + h * QB + i]
            s = s + jnp.where(lane_row < (live - c * CB) * BLK, 0.0, NEG)
            old = top_s[rows(i), :]
            top = jnp.maximum(
                old, jnp.max(jnp.maximum(s[:, :128], s[:, 128:]), axis=1, keepdims=True)
            )
            shrink = jnp.exp2((old - top) * C2)
            shift = top * C2
            parts = [jnp.exp2(s[:, t * 128 : (t + 1) * 128] * C2 - shift) for t in range(2)]
            top_s[rows(i), :] = top
            sum_s[rows(i), :] = sum_s[rows(i), :] * shrink + (parts[0] + parts[1])
            return jnp.concatenate([x.astype(jnp.bfloat16) for x in parts], axis=1), shrink

        opening = [scores(i, 0) for i in range(QB)]
        for i in range(QB):
            score_s[rows(i), :] = scores(i, 1)

        @pl.when(h == 0)
        def _():
            for copy in copies(held, v_s, 8):
                copy.wait()

        weights = [first_weights(i, s) for i, s in enumerate(opening)]
        for i, p in enumerate(weights):
            acc_s[rows(i), :] = weighted(i, 0, p)

        def chunk(c, _):
            ahead = jnp.minimum(c + 1, CHUNKS - 1)
            held = {}
            for t in range(QB + SKEW):
                if t < QB:
                    s = score_s[rows(t), :]
                    score_s[rows(t), :] = scores(t, ahead)
                    held[t] = next_weights(t, c, s)
                i = t - SKEW
                if i >= 0:
                    p, shrink = held.pop(i)
                    acc_s[rows(i), :] = acc_s[rows(i), :] * shrink + weighted(i, c, p)
            return 0

        lax.fori_loop(1, counts[h], chunk, 0)
        for i in range(QB):
            total = jnp.sum(sum_s[rows(i), :], axis=1, keepdims=True)
            o_refs[i // 2][rows(i % 2), columns] = (acc_s[rows(i), :] / total).astype(jnp.bfloat16)
        return 0

    lax.fori_loop(0, HG, head, 0)


def attend(k_lists, v_lists, counts, queries, held, swapped):
    any_space = pl.BlockSpec(memory_space=pl.ANY)
    vmem = pl.BlockSpec(memory_space=pltpu.VMEM)
    smem = pl.BlockSpec(memory_space=pltpu.SMEM)
    return pl.pallas_call(
        attend_kernel,
        out_shape=[jax.ShapeDtypeStruct((2 * BLK, HG * DH), jnp.bfloat16)] * 4,
        in_specs=[smem] * 3 + [vmem] * 4 + [any_space] * 16,
        out_specs=[vmem] * 4,
        scratch_shapes=[pltpu.VMEM((SEQ, DH), jnp.bfloat16)] * 2
        + [pltpu.VMEM((QB * BLK, DH), jnp.float32)] * 3
        + [pltpu.VMEM((QB * BLK, CB * BLK), jnp.float32), pltpu.SemaphoreType.DMA((16,))],
        compiler_params=pltpu.CompilerParams(vmem_limit_bytes=40 * 1024 * 1024),
    )(k_lists, v_lists, counts, *queries, *held, *swapped)


def place_kernel(starts, *refs):
    out_ref = refs[4]
    for n in range(4):
        columns = pl.ds(pl.multiple_of(starts[n] * (HG * DH), HG * DH), HG * DH)
        out_ref[:, columns] = refs[n][...]


def place_heads(starts, pieces):
    return pl.pallas_call(
        place_kernel,
        out_shape=jax.ShapeDtypeStruct((2 * BLK, H * DH), jnp.bfloat16),
        in_specs=[pl.BlockSpec(memory_space=pltpu.SMEM)]
        + [pl.BlockSpec(memory_space=pltpu.VMEM)] * 4,
        out_specs=pl.BlockSpec(memory_space=pltpu.VMEM),
    )(starts, *pieces)


def block_lists(own_blocks, column_blocks, column_count, slash_offsets, slash_count):
    own = jnp.tile(own_blocks, HG)[None, :]
    column = jnp.repeat(column_blocks.T, QB, axis=1)
    column_used = jnp.arange(NV, dtype=jnp.int32)[:, None] < jnp.repeat(column_count, QB)
    slash = own - jnp.repeat(slash_offsets.T, QB, axis=1)
    slash_used = jnp.arange(NS, dtype=jnp.int32)[:, None] < jnp.repeat(slash_count, QB)
    twice = jnp.any((column[None] == slash[:, None]) & column_used[None], axis=1)
    blocks = jnp.concatenate([own, column, slash])
    usable = jnp.concatenate(
        [
            jnp.ones(own.shape, bool),
            column_used & (column < own),
            slash_used & (slash >= 0) & jnp.logical_not(twice),
        ]
    )
    width = 1 + NV + NS
    earlier = jnp.arange(width)[None, :] < jnp.arange(width)[:, None]
    place = jnp.sum(usable[None] & earlier[:, :, None], axis=1, dtype=jnp.int32)
    live = jnp.sum(usable, axis=0, dtype=jnp.int32)
    slot = jnp.arange(LMAX, dtype=jnp.int32)
    chosen = usable[None] & (place[None] == slot[:, None, None])
    packed = jnp.sum(jnp.where(chosen, blocks[None], 0), axis=1)
    packed = jnp.where(slot[:, None] < live, packed, own)
    steps = (jnp.max(live.reshape(HG, QB), axis=1) + CB - 1) // CB
    return packed, steps, live


def piece_places(blocks, y, x):
    dy, dx = (blocks // 8 - y) % 4, (blocks // 2 - x) % 4
    inner = blocks // 32 * 2 + blocks % 2

    def place(small, big):
        slot = jnp.where(small < 2, 2 * small, 7 - 2 * small)
        far = slot // 2
        piece = jnp.where(
            big == 0,
            far,
            jnp.where(big == 3, 2 + 2 * far, jnp.where(big == 1, 3 + 2 * far, 6 + far)),
        )
        return piece * 64 + slot % 2 * 32 + inner

    return place(dx, dy), place(dy, dx)


def device_index(z, core, y, x):
    return ((z * 2 + core) * 4 + y) * 4 + x


def send(array, first, second=None):
    pairs = []
    for z in range(8):
        for y in range(4):
            for x in range(4):
                for core, (dz, dc, dy, dx) in enumerate((first, second or first)):
                    target = ((z + dz) % 8, core ^ dc, (y + dy) % 4, (x + dx) % 4)
                    pairs.append((device_index(z, core, y, x), device_index(*target)))
    return lax.ppermute(array, AXES, pairs)


AXES = ("z", "core", "y", "x")
UP_Y, DOWN_Y, UP_X, DOWN_X = (0, 0, 1, 0), (0, 0, -1, 0), (0, 0, 0, 1), (0, 0, 0, -1)
UP_Z, DOWN_Z, UP_2, DOWN_2 = (1, 0, 0, 0), (-1, 0, 0, 0), (2, 0, 0, 0), (-2, 0, 0, 0)
OTHER = (0, 1, 0, 0)


def gather_pairs(own, lists, late):
    up1 = send(own, UP_X, UP_Y)
    down1 = send(own, DOWN_X, DOWN_Y)
    up1, down1, lists = lax.optimization_barrier((up1, down1, lists))
    up2 = send(up1, UP_X, UP_Y)
    near = jnp.concatenate([own, up1])
    a1 = send(near, UP_Y, UP_X)
    b1 = send(near, DOWN_Y, DOWN_X)
    up2, late = lax.optimization_barrier((up2, late))
    far = jnp.concatenate([down1, up2])
    a2 = send(far, UP_Y, UP_X)
    b2 = send(far, DOWN_Y, DOWN_X)
    a3 = send(a1, UP_Y, UP_X)
    b3 = send(b2, DOWN_Y, DOWN_X)
    held = (near, far, a1, b1, a2, b2, a3, b3)
    return held, tuple(send(piece, OTHER) for piece in held), lists, late


def per_device(
    query_rows, key_rows, value_rows, column_blocks, column_count, slash_offsets, slash_count
):
    tokens = query_rows.shape[0]
    z, core, y, x = (lax.axis_index(name) for name in AXES)
    group = z % KVH
    pairs = jnp.stack(
        [array.reshape(tokens, KVH, DH).transpose(1, 0, 2) for array in (key_rows, value_rows)],
        axis=1,
    )
    own = lax.all_to_all(
        jnp.concatenate([pairs, pairs]).reshape(4 * KVH, tokens, DH),
        ("z", "core"),
        split_axis=0,
        concat_axis=0,
        tiled=True,
    ).reshape(16 * tokens, DH)

    def mine(array):
        return lax.dynamic_slice_in_dim(array, group * HG, HG, 0)

    last = jnp.where(core == 0, z + 6, z + 2)
    sources = jnp.stack([z, z + 7, z + 1, last]) % 8
    own_blocks = ((sources * 2 + core) * 32 + (y * 4 + x) * 2)[:, None] + jnp.arange(2)
    blocks, steps, live = block_lists(
        own_blocks.reshape(-1).astype(jnp.int32),
        mine(column_blocks),
        mine(column_count),
        mine(slash_offsets),
        mine(slash_count),
    )
    k_lists, v_lists = piece_places(blocks, y, x)
    counts = jnp.concatenate([steps, live, core[None]])
    lists = (k_lists.reshape(-1), v_lists.reshape(-1), counts)
    held, swapped, lists, query_rows = gather_pairs(own, lists, query_rows)

    def heads(step):
        start = (z + step) % KVH * (HG * DH)
        return lax.dynamic_slice_in_dim(query_rows, start, HG * DH, 1)

    queries = (
        heads(0),
        send(heads(1), UP_Z),
        send(heads(3), DOWN_Z),
        send(heads(2), UP_2, DOWN_2),
    )
    outputs = attend(*lists, queries, held, swapped)
    pieces = (
        outputs[0],
        send(outputs[1], DOWN_Z),
        send(outputs[2], UP_Z),
        send(outputs[3], DOWN_2, UP_2),
    )
    starts = jnp.stack([z, z + 1, z + 3, z + 2]) % KVH
    return place_heads(starts.astype(jnp.int32), pieces)


def solution(mesh):
    fine = Mesh(mesh.devices.reshape(8, 2, 4, 4), AXES)
    split = P(AXES, None)
    return jax.shard_map(
        per_device,
        mesh=fine,
        in_specs=(split, split, split, P(), P(), P(), P()),
        out_specs=split,
        check_vma=False,
    )
```

```python
import math

import jax
import jax.numpy as jnp
from jax import lax
from jax.experimental import pallas as pl
from jax.experimental.pallas import tpu as pltpu
from jax.sharding import Mesh, PartitionSpec as P

H = 32
KVH = 4
DH = 128
BLK = 64
NV = 8
NS = 24
SEQ = 32768

QB = 8
HG = H // KVH
CB = 4
CHUNKS = -(-(1 + NV + NS) // CB)
LMAX = CHUNKS * CB
SKEW = 4
C2 = math.log2(math.e) / math.sqrt(DH)
NEG = -1e30
NT = (((1,), (1,)), ((), ()))
PIECE = SEQ // 8


def attend_kernel(k_lists, v_lists, counts, *refs):
    q_refs, held, swapped, o_refs = refs[:4], refs[4:9], refs[9:14], refs[14:18]
    k_s, v_s, top_s, sum_s, acc_s, score_s, sem = refs[18:]
    is_first = counts[HG + HG * QB] == 0

    def copies(source, target, first_sem):
        return [
            pltpu.make_async_copy(
                piece, target.at[pl.ds(start * PIECE, piece.shape[0]), :], sem.at[first_sem + p]
            )
            for p, (piece, start) in enumerate(zip(source, (0, 2, 4, 6, 7)))
        ]

    @pl.when(is_first)
    def _():
        for copy in copies(held, k_s, 0) + copies(swapped, v_s, 8):
            copy.start()

    @pl.when(jnp.logical_not(is_first))
    def _():
        for copy in copies(swapped, k_s, 0) + copies(held, v_s, 8):
            copy.start()

    for copy in copies(held, k_s, 0):
        copy.wait()
    lane = lax.broadcasted_iota(jnp.int32, (BLK, CB * BLK), 1)
    row = lax.broadcasted_iota(jnp.int32, (BLK, CB * BLK), 0)
    lane_row = lax.broadcasted_iota(jnp.int32, (1, CB * BLK), 1)

    def rows(i):
        return slice(i * BLK, (i + 1) * BLK)

    def head(h, _):
        columns = pl.ds(pl.multiple_of(h * DH, DH), DH)

        def gather(ref, lists, i, c):
            base = c * (CB * HG * QB) + (h * QB + i)
            return jnp.concatenate(
                [
                    ref[pl.ds(pl.multiple_of(lists[base + j * (HG * QB)] * BLK, BLK), BLK), :]
                    for j in range(CB)
                ],
                axis=0,
            )

        def scores(i, c):
            return lax.dot_general(
                q_refs[i // 2][rows(i % 2), columns],
                gather(k_s, k_lists, i, c),
                NT,
                preferred_element_type=jnp.float32,
            )

        def weighted(i, c, p):
            return jnp.dot(p, gather(v_s, v_lists, i, c), preferred_element_type=jnp.float32)

        def first_weights(i, s):
            live = counts[HG + h * QB + i]
            s = jnp.where((lane < live * BLK) & ((lane >= BLK) | (lane <= row)), s, NEG)
            top = jnp.max(jnp.maximum(s[:, :128], s[:, 128:]), axis=1, keepdims=True)
            shift = top * C2
            parts = [jnp.exp2(s[:, t * 128 : (t + 1) * 128] * C2 - shift) for t in range(2)]
            top_s[rows(i), :] = jnp.broadcast_to(top, (BLK, DH))
            sum_s[rows(i), :] = parts[0] + parts[1]
            return jnp.concatenate([x.astype(jnp.bfloat16) for x in parts], axis=1)

        def next_weights(i, c, s):
            live = counts[HG + h * QB + i]
            s = s + jnp.where(lane_row < (live - c * CB) * BLK, 0.0, NEG)
            old = top_s[rows(i), :]
            top = jnp.maximum(
                old, jnp.max(jnp.maximum(s[:, :128], s[:, 128:]), axis=1, keepdims=True)
            )
            shrink = jnp.exp2((old - top) * C2)
            shift = top * C2
            parts = [jnp.exp2(s[:, t * 128 : (t + 1) * 128] * C2 - shift) for t in range(2)]
            top_s[rows(i), :] = top
            sum_s[rows(i), :] = sum_s[rows(i), :] * shrink + (parts[0] + parts[1])
            return jnp.concatenate([x.astype(jnp.bfloat16) for x in parts], axis=1), shrink

        opening = [scores(i, 0) for i in range(QB)]
        for i in range(QB):
            score_s[rows(i), :] = scores(i, 1)

        @pl.when(h == 0)
        def _():
            for copy in copies(held, v_s, 8):
                copy.wait()

        weights = [first_weights(i, s) for i, s in enumerate(opening)]
        for i, p in enumerate(weights):
            acc_s[rows(i), :] = weighted(i, 0, p)

        def chunk(c, _):
            ahead = jnp.minimum(c + 1, CHUNKS - 1)
            held = {}
            for t in range(QB + SKEW):
                if t < QB:
                    s = score_s[rows(t), :]
                    score_s[rows(t), :] = scores(t, ahead)
                    held[t] = next_weights(t, c, s)
                i = t - SKEW
                if i >= 0:
                    p, shrink = held.pop(i)
                    acc_s[rows(i), :] = acc_s[rows(i), :] * shrink + weighted(i, c, p)
            return 0

        lax.fori_loop(1, counts[h], chunk, 0)
        for i in range(QB):
            total = jnp.sum(sum_s[rows(i), :], axis=1, keepdims=True)
            o_refs[i // 2][rows(i % 2), columns] = (acc_s[rows(i), :] / total).astype(jnp.bfloat16)
        return 0

    lax.fori_loop(0, HG, head, 0)


def attend(k_lists, v_lists, counts, queries, held, swapped):
    any_space = pl.BlockSpec(memory_space=pl.ANY)
    vmem = pl.BlockSpec(memory_space=pltpu.VMEM)
    smem = pl.BlockSpec(memory_space=pltpu.SMEM)
    return pl.pallas_call(
        attend_kernel,
        out_shape=[jax.ShapeDtypeStruct((2 * BLK, HG * DH), jnp.bfloat16)] * 4,
        in_specs=[smem] * 3 + [vmem] * 4 + [any_space] * 10,
        out_specs=[vmem] * 4,
        scratch_shapes=[pltpu.VMEM((SEQ, DH), jnp.bfloat16)] * 2
        + [pltpu.VMEM((QB * BLK, DH), jnp.float32)] * 3
        + [pltpu.VMEM((QB * BLK, CB * BLK), jnp.float32), pltpu.SemaphoreType.DMA((16,))],
        compiler_params=pltpu.CompilerParams(vmem_limit_bytes=40 * 1024 * 1024),
    )(k_lists, v_lists, counts, *queries, *held, *swapped)


def place_kernel(starts, *refs):
    out_ref = refs[4]
    for n in range(4):
        columns = pl.ds(pl.multiple_of(starts[n] * (HG * DH), HG * DH), HG * DH)
        out_ref[:, columns] = refs[n][...]


def place_heads(starts, pieces):
    return pl.pallas_call(
        place_kernel,
        out_shape=jax.ShapeDtypeStruct((2 * BLK, H * DH), jnp.bfloat16),
        in_specs=[pl.BlockSpec(memory_space=pltpu.SMEM)]
        + [pl.BlockSpec(memory_space=pltpu.VMEM)] * 4,
        out_specs=pl.BlockSpec(memory_space=pltpu.VMEM),
    )(starts, *pieces)


def block_lists(own_blocks, column_blocks, column_count, slash_offsets, slash_count):
    own = jnp.tile(own_blocks, HG)[None, :]
    column = jnp.repeat(column_blocks.T, QB, axis=1)
    column_used = jnp.arange(NV, dtype=jnp.int32)[:, None] < jnp.repeat(column_count, QB)
    slash = own - jnp.repeat(slash_offsets.T, QB, axis=1)
    slash_used = jnp.arange(NS, dtype=jnp.int32)[:, None] < jnp.repeat(slash_count, QB)
    twice = jnp.any((column[None] == slash[:, None]) & column_used[None], axis=1)
    blocks = jnp.concatenate([own, column, slash])
    usable = jnp.concatenate(
        [
            jnp.ones(own.shape, bool),
            column_used & (column < own),
            slash_used & (slash >= 0) & jnp.logical_not(twice),
        ]
    )
    width = 1 + NV + NS
    earlier = jnp.arange(width)[None, :] < jnp.arange(width)[:, None]
    place = jnp.sum(usable[None] & earlier[:, :, None], axis=1, dtype=jnp.int32)
    live = jnp.sum(usable, axis=0, dtype=jnp.int32)
    slot = jnp.arange(LMAX, dtype=jnp.int32)
    chosen = usable[None] & (place[None] == slot[:, None, None])
    packed = jnp.sum(jnp.where(chosen, blocks[None], 0), axis=1)
    packed = jnp.where(slot[:, None] < live, packed, own)
    steps = (jnp.max(live.reshape(HG, QB), axis=1) + CB - 1) // CB
    return packed, steps, live


def piece_places(blocks, y, x):
    dy, dx = (blocks // 8 - y) % 4, (blocks // 2 - x) % 4
    inner = blocks // 32 * 2 + blocks % 2

    def place(small, big):
        slot = jnp.where(small < 2, 2 * small, 7 - 2 * small)
        far = slot // 2
        piece = jnp.where(
            big == 0,
            far,
            jnp.where(big == 3, 2 + far, jnp.where(big == 1, 4 + far, 6 + far)),
        )
        return piece * 64 + slot % 2 * 32 + inner

    return place(dx, dy), place(dy, dx)


def device_index(z, core, y, x):
    return ((z * 2 + core) * 4 + y) * 4 + x


def send(array, first, second=None):
    pairs = []
    for z in range(8):
        for y in range(4):
            for x in range(4):
                for core, (dz, dc, dy, dx) in enumerate((first, second or first)):
                    target = ((z + dz) % 8, core ^ dc, (y + dy) % 4, (x + dx) % 4)
                    pairs.append((device_index(z, core, y, x), device_index(*target)))
    return lax.ppermute(array, AXES, pairs)


AXES = ("z", "core", "y", "x")
UP_Y, DOWN_Y, UP_X, DOWN_X = (0, 0, 1, 0), (0, 0, -1, 0), (0, 0, 0, 1), (0, 0, 0, -1)
UP_Z, DOWN_Z, UP_2, DOWN_2 = (1, 0, 0, 0), (-1, 0, 0, 0), (2, 0, 0, 0), (-2, 0, 0, 0)
OTHER = (0, 1, 0, 0)


def gather_pairs(own, lists, late):
    tie = lax.optimization_barrier
    own, late = tie((own, late))
    up1 = send(own, UP_X, UP_Y)
    down1 = send(own, DOWN_X, DOWN_Y)
    up2 = send(own, (0, 0, 0, 2), (0, 0, 2, 0))
    queries = (late[0], send(late[1], UP_Z), send(late[2], DOWN_Z), send(late[3], UP_2, DOWN_2))
    up1, down1, up2, lists = tie((up1, down1, up2, lists))
    near = jnp.concatenate([own, up1, down1, up2])
    a1 = send(near, UP_Y, UP_X)
    b1 = send(near, DOWN_Y, DOWN_X)
    a2 = send(a1[:PIECE], UP_Y, UP_X)
    b2 = send(b1[PIECE:], DOWN_Y, DOWN_X)
    held = (near, a1, b1, a2, b2)
    return held, tuple(send(piece, OTHER) for piece in held), lists, queries


def per_device(
    query_rows, key_rows, value_rows, column_blocks, column_count, slash_offsets, slash_count
):
    tokens = query_rows.shape[0]
    z, core, y, x = (lax.axis_index(name) for name in AXES)
    group = z % KVH
    pairs = jnp.stack(
        [array.reshape(tokens, KVH, DH).transpose(1, 0, 2) for array in (key_rows, value_rows)],
        axis=1,
    )
    own = lax.all_to_all(
        jnp.concatenate([pairs, pairs]).reshape(4 * KVH, tokens, DH),
        ("z", "core"),
        split_axis=0,
        concat_axis=0,
        tiled=True,
    ).reshape(16 * tokens, DH)

    def mine(array):
        return lax.dynamic_slice_in_dim(array, group * HG, HG, 0)

    last = jnp.where(core == 0, z + 6, z + 2)
    sources = jnp.stack([z, z + 7, z + 1, last]) % 8
    own_blocks = ((sources * 2 + core) * 32 + (y * 4 + x) * 2)[:, None] + jnp.arange(2)
    blocks, steps, live = block_lists(
        own_blocks.reshape(-1).astype(jnp.int32),
        mine(column_blocks),
        mine(column_count),
        mine(slash_offsets),
        mine(slash_count),
    )
    k_lists, v_lists = piece_places(blocks, y, x)
    counts = jnp.concatenate([steps, live, core[None]])
    lists = (k_lists.reshape(-1), v_lists.reshape(-1), counts)
    def heads(step):
        start = (z + step) % KVH * (HG * DH)
        return lax.dynamic_slice_in_dim(query_rows, start, HG * DH, 1)

    late = (heads(0), heads(1), heads(3), heads(2))
    held, swapped, lists, queries = gather_pairs(own, lists, late)
    outputs = attend(*lists, queries, held, swapped)
    pieces = (
        outputs[0],
        send(outputs[1], DOWN_Z),
        send(outputs[2], UP_Z),
        send(outputs[3], DOWN_2, UP_2),
    )
    starts = jnp.stack([z, z + 1, z + 3, z + 2]) % KVH
    return place_heads(starts.astype(jnp.int32), pieces)


def solution(mesh):
    fine = Mesh(mesh.devices.reshape(8, 2, 4, 4), AXES)
    split = P(AXES, None)
    return jax.shard_map(
        per_device,
        mesh=fine,
        in_specs=(split, split, split, P(), P(), P(), P()),
        out_specs=split,
        check_vma=False,
    )
```

```python
import functools
import math

import jax
import jax.numpy as jnp
from jax import lax
from jax.experimental import pallas as pl
from jax.experimental.pallas import tpu as pltpu
from jax.sharding import Mesh, PartitionSpec as P

H = 32
KVH = 4
DH = 128
BLK = 64
NV = 8
NS = 24
SEQ = 32768

QB = 8
HG = H // KVH
CB = 4
CHUNKS = -(-(1 + NV + NS) // CB)
LMAX = CHUNKS * CB
SKEW = 4
C2 = math.log2(math.e) / math.sqrt(DH)
NEG = -1e30
NT = (((1,), (1,)), ((), ()))
LIMIT = 8 * 1024 * 1024
PARTS = 2
PIECE = 4 * 2048
ITEMS = HG * QB
STATE = 3 * (jax.ShapeDtypeStruct((ITEMS * BLK, DH), jnp.float32),)
VMEM = pl.BlockSpec(memory_space=pltpu.VMEM)
SMEM = pl.BlockSpec(memory_space=pltpu.SMEM)
ANY = pl.BlockSpec(memory_space=pl.ANY)


def collect_kernel(starts, count, first, *refs):
    held, swapped = refs[:count], refs[count : 2 * count]
    buffer, sem = refs[2 * count + (0 if first else 1) :]
    copies = []
    for p in range(count):
        for other, piece in enumerate((held[p], swapped[p])):
            place = pl.ds(other * 4 * PIECE + starts[p], piece.shape[0])
            copies.append(pltpu.make_async_copy(piece, buffer.at[place, :], sem.at[len(copies)]))
    for copy in copies:
        copy.start()
    for copy in copies:
        copy.wait()


def collect(held, starts, buffer):
    swapped = [send(piece, OTHER) for piece in held]
    count = len(held)
    return pl.pallas_call(
        functools.partial(collect_kernel, starts, count, not buffer),
        out_shape=[jax.ShapeDtypeStruct((8 * PIECE, DH), jnp.bfloat16)],
        in_specs=[ANY] * (2 * count) + [VMEM] * len(buffer),
        out_specs=[VMEM],
        scratch_shapes=[pltpu.SemaphoreType.DMA((2 * count,))],
        input_output_aliases={2 * count: 0} if buffer else {},
        compiler_params=pltpu.CompilerParams(vmem_limit_bytes=LIMIT),
    )(*held, *swapped, *buffer)


def attend_kernel(part, lists, counts, *refs):
    q_refs, pairs = refs[:4], refs[4]
    refs = refs[5:] if part == 0 else refs[8:]
    top_s, sum_s, acc_s = refs[:3]
    o_refs, score_s = refs[3:-1], refs[-1]
    first_list, first_count = part * LMAX * ITEMS, part * (HG + ITEMS)
    lane = lax.broadcasted_iota(jnp.int32, (BLK, CB * BLK), 1)
    row = lax.broadcasted_iota(jnp.int32, (BLK, CB * BLK), 0)
    lane_row = lax.broadcasted_iota(jnp.int32, (1, CB * BLK), 1)

    def rows(i):
        return slice(i * BLK, (i + 1) * BLK)

    def head(h, _):
        columns = pl.ds(pl.multiple_of(h * DH, DH), DH)

        def state(i):
            return pl.ds(pl.multiple_of((h * QB + i) * BLK, BLK), BLK)

        def live(i):
            return counts[first_count + HG + h * QB + i]

        def gather(i, c, ahead):
            base = first_list + c * (CB * ITEMS) + (h * QB + i)
            return jnp.concatenate(
                [
                    pairs[
                        pl.ds(
                            pl.multiple_of((lists[base + j * ITEMS] + ahead) * BLK, BLK), BLK
                        ),
                        :,
                    ]
                    for j in range(CB)
                ],
                axis=0,
            )

        def scores(i, c):
            return lax.dot_general(
                q_refs[i // 2][rows(i % 2), columns],
                gather(i, c, 0),
                NT,
                preferred_element_type=jnp.float32,
            )

        def weighted(i, c, p):
            return jnp.dot(p, gather(i, c, 2), preferred_element_type=jnp.float32)

        def first_weights(i, s):
            s = jnp.where((lane < live(i) * BLK) & ((lane >= BLK) | (lane <= row)), s, NEG)
            top = jnp.max(jnp.maximum(s[:, :128], s[:, 128:]), axis=1, keepdims=True)
            shift = top * C2
            parts = [jnp.exp2(s[:, t * 128 : (t + 1) * 128] * C2 - shift) for t in range(2)]
            top_s[state(i), :] = jnp.broadcast_to(top, (BLK, DH))
            sum_s[state(i), :] = parts[0] + parts[1]
            return jnp.concatenate([x.astype(jnp.bfloat16) for x in parts], axis=1)

        def next_weights(i, c, s):
            s = s + jnp.where(lane_row < (live(i) - c * CB) * BLK, 0.0, NEG)
            old = top_s[state(i), :]
            top = jnp.maximum(
                old, jnp.max(jnp.maximum(s[:, :128], s[:, 128:]), axis=1, keepdims=True)
            )
            shrink = jnp.exp2((old - top) * C2)
            shift = top * C2
            parts = [jnp.exp2(s[:, t * 128 : (t + 1) * 128] * C2 - shift) for t in range(2)]
            top_s[state(i), :] = top
            sum_s[state(i), :] = sum_s[state(i), :] * shrink + (parts[0] + parts[1])
            return jnp.concatenate([x.astype(jnp.bfloat16) for x in parts], axis=1), shrink

        first_chunk = 1 if part == 0 else 0
        if part == 0:
            opening = [scores(i, 0) for i in range(QB)]
        for i in range(QB):
            score_s[rows(i), :] = scores(i, first_chunk)
        if part == 0:
            weights = [first_weights(i, s) for i, s in enumerate(opening)]
            for i, p in enumerate(weights):
                acc_s[state(i), :] = weighted(i, 0, p)

        def chunk(c, _):
            ahead = jnp.minimum(c + 1, CHUNKS - 1)
            held = {}
            for t in range(QB + SKEW):
                if t < QB:
                    s = score_s[rows(t), :]
                    score_s[rows(t), :] = scores(t, ahead)
                    held[t] = next_weights(t, c, s)
                i = t - SKEW
                if i >= 0:
                    p, shrink = held.pop(i)
                    acc_s[state(i), :] = acc_s[state(i), :] * shrink + weighted(i, c, p)
            return 0

        lax.fori_loop(first_chunk, counts[first_count + h], chunk, 0)
        for i in range(QB if o_refs else 0):
            total = jnp.sum(sum_s[state(i), :], axis=1, keepdims=True)
            o_refs[i // 2][rows(i % 2), columns] = (acc_s[state(i), :] / total).astype(
                jnp.bfloat16
            )
        return 0

    lax.fori_loop(0, HG, head, 0)


def attend(part, lists, counts, queries, buffer, state):
    outputs = [jax.ShapeDtypeStruct((2 * BLK, HG * DH), jnp.bfloat16)] * (4 if part == PARTS - 1 else 0)
    return pl.pallas_call(
        functools.partial(attend_kernel, part),
        out_shape=list(STATE) + outputs,
        in_specs=[SMEM] * 2 + [VMEM] * (5 + len(state)),
        out_specs=[VMEM] * (3 + len(outputs)),
        scratch_shapes=[pltpu.VMEM((QB * BLK, CB * BLK), jnp.float32)],
        input_output_aliases={7 + n: n for n in range(len(state))},
        compiler_params=pltpu.CompilerParams(vmem_limit_bytes=LIMIT),
        cost_estimate=pl.CostEstimate(
            flops=3_000_000_000, bytes_accessed=30_000_000, transcendentals=3_000_000
        ),
    )(lists, counts, *queries, *buffer, *state)


def place_kernel(starts, *refs):
    out_ref = refs[4]
    for n in range(4):
        columns = pl.ds(pl.multiple_of(starts[n] * (HG * DH), HG * DH), HG * DH)
        out_ref[:, columns] = refs[n][...]


def place_heads(starts, pieces):
    return pl.pallas_call(
        place_kernel,
        out_shape=jax.ShapeDtypeStruct((2 * BLK, H * DH), jnp.bfloat16),
        in_specs=[pl.BlockSpec(memory_space=pltpu.SMEM)]
        + [pl.BlockSpec(memory_space=pltpu.VMEM)] * 4,
        out_specs=pl.BlockSpec(memory_space=pltpu.VMEM),
    )(starts, *pieces)


def piece_places(blocks, core, y, x):
    dy, dx = (blocks // 8 - y) % 4, (blocks // 2 - x) % 4
    half = blocks // 32 % 2
    small, big = jnp.where(half == 0, dx, dy), jnp.where(half == 0, dy, dx)

    def ring(d):
        return jnp.where(d < 2, 2 * d, 7 - 2 * d)

    inner = blocks // 64 * 4 + blocks % 2
    places = jnp.where(half == core, 0, 512) + ring(big) * 128 + ring(small) * 32 + inner
    return places, jnp.where(big == 0, 0, 1)


def block_lists(place_of, own_blocks, column_blocks, column_count, slash_offsets, slash_count):
    own = jnp.tile(own_blocks, HG)[None, :]
    column = jnp.repeat(column_blocks.T, QB, axis=1)
    column_used = jnp.arange(NV, dtype=jnp.int32)[:, None] < jnp.repeat(column_count, QB)
    slash = own - jnp.repeat(slash_offsets.T, QB, axis=1)
    slash_used = jnp.arange(NS, dtype=jnp.int32)[:, None] < jnp.repeat(slash_count, QB)
    twice = jnp.any((column[None] == slash[:, None]) & column_used[None], axis=1)
    blocks = jnp.concatenate([own, column, jnp.maximum(slash, 0)])
    usable = jnp.concatenate(
        [
            jnp.ones(own.shape, bool),
            column_used & (column < own),
            slash_used & (slash >= 0) & jnp.logical_not(twice),
        ]
    )
    places, parts = place_of(blocks)
    width = 1 + NV + NS
    earlier = (jnp.arange(width)[None, :] < jnp.arange(width)[:, None])[:, :, None]
    slot = jnp.arange(LMAX, dtype=jnp.int32)[:, None, None]
    lists, counts = [], []
    for part in range(PARTS):
        used = usable & (parts == part)
        rank = jnp.sum(used[None] & earlier, axis=1, dtype=jnp.int32)
        live = jnp.sum(used, axis=0, dtype=jnp.int32)
        packed = jnp.where(used[None] & (rank[None] == slot), places[None], 0)
        lists.append(jnp.sum(packed, axis=1))
        counts.append((jnp.max(live.reshape(HG, QB), axis=1) + CB - 1) // CB)
        counts.append(live)
    return jnp.concatenate(lists).reshape(-1), jnp.concatenate(counts)


def device_index(z, core, y, x):
    return ((z * 2 + core) * 4 + y) * 4 + x


def send(array, first, second=None):
    pairs = []
    for z in range(8):
        for y in range(4):
            for x in range(4):
                for core, (dz, dc, dy, dx) in enumerate((first, second or first)):
                    target = ((z + dz) % 8, core ^ dc, (y + dy) % 4, (x + dx) % 4)
                    pairs.append((device_index(z, core, y, x), device_index(*target)))
    return lax.ppermute(array, AXES, pairs)


AXES = ("z", "core", "y", "x")
UP_Y, DOWN_Y, UP_X, DOWN_X = (0, 0, 1, 0), (0, 0, -1, 0), (0, 0, 0, 1), (0, 0, 0, -1)
UP_Z, DOWN_Z, UP_2, DOWN_2 = (1, 0, 0, 0), (-1, 0, 0, 0), (2, 0, 0, 0), (-2, 0, 0, 0)
OTHER = (0, 1, 0, 0)


def gather_and_attend(own, lists, counts, late):
    tie = lax.optimization_barrier
    own, late = tie((own, late))
    up1 = send(own, UP_X, UP_Y)
    down1 = send(own, DOWN_X, DOWN_Y)
    up2 = send(own, (0, 0, 0, 2), (0, 0, 2, 0))
    near_queries = (late[0], send(late[1], UP_Z), send(late[2], DOWN_Z))
    up1, down1, up2, lists, counts, near_queries, far_query = tie(
        (up1, down1, up2, lists, counts, near_queries, late[3])
    )
    queries = near_queries + (send(far_query, UP_2, DOWN_2),)
    near = jnp.concatenate([own, up1, down1, up2])
    a1 = send(near, UP_Y, UP_X)
    b1 = send(near, DOWN_Y, DOWN_X)
    buffer = collect([near], [0], ())
    state = attend(0, lists, counts, queries, buffer, ())
    a1, b1, buffer, state = tie((a1, b1, buffer, state))
    a2 = send(a1[: PIECE // 2], UP_Y, UP_X)
    b2 = send(b1[PIECE // 2 :], DOWN_Y, DOWN_X)
    buffer = collect([a1, b1], [PIECE, 2 * PIECE], buffer)
    a2, b2, buffer = tie((a2, b2, buffer))
    buffer = collect([a2, b2], [3 * PIECE, 3 * PIECE + PIECE // 2], buffer)
    return attend(1, lists, counts, queries, buffer, state)[3:]


def per_device(
    query_rows, key_rows, value_rows, column_blocks, column_count, slash_offsets, slash_count
):
    tokens = query_rows.shape[0]
    z, core, y, x = (lax.axis_index(name) for name in AXES)
    group = z % KVH
    pairs = jnp.stack(
        [array.reshape(tokens, KVH, DH).transpose(1, 0, 2) for array in (key_rows, value_rows)],
        axis=1,
    )
    own = lax.all_to_all(
        jnp.concatenate([pairs, pairs]), "z", split_axis=0, concat_axis=0, tiled=True
    ).reshape(16 * tokens, DH)

    def mine(array):
        return lax.dynamic_slice_in_dim(array, group * HG, HG, 0)

    last = jnp.where(core == 0, z + 6, z + 2)
    sources = jnp.stack([z, z + 7, z + 1, last]) % 8
    own_blocks = ((sources * 2 + core) * 32 + (y * 4 + x) * 2)[:, None] + jnp.arange(2)
    lists, counts = block_lists(
        functools.partial(piece_places, core=core, y=y, x=x),
        own_blocks.reshape(-1).astype(jnp.int32),
        mine(column_blocks),
        mine(column_count),
        mine(slash_offsets),
        mine(slash_count),
    )

    def heads(step):
        start = (z + step) % KVH * (HG * DH)
        return lax.dynamic_slice_in_dim(query_rows, start, HG * DH, 1)

    late = (heads(0), heads(1), heads(3), heads(2))
    outputs = gather_and_attend(own, lists, counts, late)
    pieces = (
        outputs[0],
        send(outputs[1], DOWN_Z),
        send(outputs[2], UP_Z),
        send(outputs[3], DOWN_2, UP_2),
    )
    starts = jnp.stack([z, z + 1, z + 3, z + 2]) % KVH
    return place_heads(starts.astype(jnp.int32), pieces)


def solution(mesh):
    fine = Mesh(mesh.devices.reshape(8, 2, 4, 4), AXES)
    split = P(AXES, None)
    return jax.shard_map(
        per_device,
        mesh=fine,
        in_specs=(split, split, split, P(), P(), P(), P()),
        out_specs=split,
        check_vma=False,
    )
```

```python
import functools
import math

import jax
import jax.numpy as jnp
from jax import lax
from jax.experimental import pallas as pl
from jax.experimental.pallas import tpu as pltpu
from jax.sharding import Mesh, PartitionSpec as P

H = 32
KVH = 4
DH = 128
BLK = 64
NV = 8
NS = 24
SEQ = 32768

QB = 8
HG = H // KVH
CB = 4
CHUNKS = -(-(1 + NV + NS) // CB)
LMAX = CHUNKS * CB
SKEW = 4
C2 = math.log2(math.e) / math.sqrt(DH)
NEG = -1e30
NT = (((1,), (1,)), ((), ()))
LIMIT = 8 * 1024 * 1024
PARTS = 2
PIECE = 4 * 2048
ITEMS = HG * QB
STATE = 3 * (jax.ShapeDtypeStruct((ITEMS * BLK, DH), jnp.float32),)
VMEM = pl.BlockSpec(memory_space=pltpu.VMEM)
SMEM = pl.BlockSpec(memory_space=pltpu.SMEM)
ANY = pl.BlockSpec(memory_space=pl.ANY)


def collect_kernel(starts, count, first, *refs):
    held, swapped = refs[:count], refs[count : 2 * count]
    buffer, sem = refs[2 * count + (0 if first else 1) :]
    copies = []
    for p in range(count):
        for other, piece in enumerate((held[p], swapped[p])):
            place = pl.ds(other * 4 * PIECE + starts[p], piece.shape[0])
            copies.append(pltpu.make_async_copy(piece, buffer.at[place, :], sem.at[len(copies)]))
    for copy in copies:
        copy.start()
    for copy in copies:
        copy.wait()


def collect(held, starts, buffer):
    swapped = [send(piece, OTHER) for piece in held]
    count = len(held)
    return pl.pallas_call(
        functools.partial(collect_kernel, starts, count, not buffer),
        out_shape=[jax.ShapeDtypeStruct((8 * PIECE, DH), jnp.bfloat16)],
        in_specs=[ANY] * (2 * count) + [VMEM] * len(buffer),
        out_specs=[VMEM],
        scratch_shapes=[pltpu.SemaphoreType.DMA((2 * count,))],
        input_output_aliases={2 * count: 0} if buffer else {},
        compiler_params=pltpu.CompilerParams(vmem_limit_bytes=LIMIT),
    )(*held, *swapped, *buffer)


def attend_kernel(part, lists, counts, *refs):
    q_refs, pairs = refs[:4], refs[4]
    refs = refs[5:] if part == 0 else refs[8:]
    top_s, sum_s, acc_s = refs[:3]
    o_refs, score_s = refs[3:-1], refs[-1]
    first_list, first_count = part * LMAX * ITEMS, part * (HG + ITEMS)
    lane = lax.broadcasted_iota(jnp.int32, (BLK, CB * BLK), 1)
    row = lax.broadcasted_iota(jnp.int32, (BLK, CB * BLK), 0)
    lane_row = lax.broadcasted_iota(jnp.int32, (1, CB * BLK), 1)

    def rows(i):
        return slice(i * BLK, (i + 1) * BLK)

    def head(h, _):
        columns = pl.ds(pl.multiple_of(h * DH, DH), DH)

        def state(i):
            return pl.ds(pl.multiple_of((h * QB + i) * BLK, BLK), BLK)

        def live(i):
            return counts[first_count + HG + h * QB + i]

        def gather(i, c, ahead, g=h):
            base = first_list + c * (CB * ITEMS) + (g * QB + i)
            return jnp.concatenate(
                [
                    pairs[
                        pl.ds(
                            pl.multiple_of((lists[base + j * ITEMS] + ahead) * BLK, BLK), BLK
                        ),
                        :,
                    ]
                    for j in range(CB)
                ],
                axis=0,
            )

        def scores(i, c, g=h):
            return lax.dot_general(
                q_refs[i // 2][rows(i % 2), pl.ds(pl.multiple_of(g * DH, DH), DH)],
                gather(i, c, 0, g),
                NT,
                preferred_element_type=jnp.float32,
            )

        def weighted(i, c, p):
            return jnp.dot(p, gather(i, c, 2), preferred_element_type=jnp.float32)

        def first_weights(i, s):
            s = jnp.where((lane < live(i) * BLK) & ((lane >= BLK) | (lane <= row)), s, NEG)
            top = jnp.max(jnp.maximum(s[:, :128], s[:, 128:]), axis=1, keepdims=True)
            shift = top * C2
            parts = [jnp.exp2(s[:, t * 128 : (t + 1) * 128] * C2 - shift) for t in range(2)]
            top_s[state(i), :] = jnp.broadcast_to(top, (BLK, DH))
            sum_s[state(i), :] = parts[0] + parts[1]
            return jnp.concatenate([x.astype(jnp.bfloat16) for x in parts], axis=1)

        def next_weights(i, c, s):
            s = s + jnp.where(lane_row < (live(i) - c * CB) * BLK, 0.0, NEG)
            old = top_s[state(i), :]
            top = jnp.maximum(
                old, jnp.max(jnp.maximum(s[:, :128], s[:, 128:]), axis=1, keepdims=True)
            )
            shrink = jnp.exp2((old - top) * C2)
            shift = top * C2
            parts = [jnp.exp2(s[:, t * 128 : (t + 1) * 128] * C2 - shift) for t in range(2)]
            top_s[state(i), :] = top
            sum_s[state(i), :] = sum_s[state(i), :] * shrink + (parts[0] + parts[1])
            return jnp.concatenate([x.astype(jnp.bfloat16) for x in parts], axis=1), shrink

        first_chunk = 1 if part == 0 else 0
        chunks = counts[first_count + h]
        if part == 0:
            opening = [scores(i, 0) for i in range(QB)]
            for i in range(QB):
                score_s[rows(i), :] = scores(i, first_chunk)
        else:
            chunks = jnp.maximum(chunks, 1)

            @pl.when(h == 0)
            def _():
                for i in range(QB):
                    score_s[rows(i), :] = scores(i, 0)

        if part == 0:
            weights = [first_weights(i, s) for i, s in enumerate(opening)]
            for i, p in enumerate(weights):
                acc_s[state(i), :] = weighted(i, 0, p)

        def chunk(c, _):
            ahead, next_head = jnp.minimum(c + 1, CHUNKS - 1), h
            if part:
                ahead = jnp.where(c + 1 < chunks, c + 1, 0)
                next_head = jnp.where(c + 1 < chunks, h, jnp.minimum(h + 1, HG - 1))
            held = {}
            for t in range(QB + SKEW):
                if t < QB:
                    s = score_s[rows(t), :]
                    score_s[rows(t), :] = scores(t, ahead, next_head)
                    held[t] = next_weights(t, c, s)
                i = t - SKEW
                if i >= 0:
                    p, shrink = held.pop(i)
                    acc_s[state(i), :] = acc_s[state(i), :] * shrink + weighted(i, c, p)
            return 0

        lax.fori_loop(first_chunk, chunks, chunk, 0)
        for i in range(QB if o_refs else 0):
            total = jnp.sum(sum_s[state(i), :], axis=1, keepdims=True)
            o_refs[i // 2][rows(i % 2), columns] = (acc_s[state(i), :] / total).astype(
                jnp.bfloat16
            )
        return 0

    lax.fori_loop(0, HG, head, 0)


def attend(part, lists, counts, queries, buffer, state):
    outputs = [jax.ShapeDtypeStruct((2 * BLK, HG * DH), jnp.bfloat16)] * (4 if part == PARTS - 1 else 0)
    return pl.pallas_call(
        functools.partial(attend_kernel, part),
        out_shape=list(STATE) + outputs,
        in_specs=[SMEM] * 2 + [VMEM] * (5 + len(state)),
        out_specs=[VMEM] * (3 + len(outputs)),
        scratch_shapes=[pltpu.VMEM((QB * BLK, CB * BLK), jnp.float32)],
        input_output_aliases={7 + n: n for n in range(len(state))},
        compiler_params=pltpu.CompilerParams(vmem_limit_bytes=LIMIT),
        cost_estimate=pl.CostEstimate(
            flops=3_000_000_000, bytes_accessed=30_000_000, transcendentals=3_000_000
        ),
    )(lists, counts, *queries, *buffer, *state)


def place_kernel(starts, *refs):
    out_ref = refs[4]
    for n in range(4):
        columns = pl.ds(pl.multiple_of(starts[n] * (HG * DH), HG * DH), HG * DH)
        out_ref[:, columns] = refs[n][...]


def place_heads(starts, pieces):
    return pl.pallas_call(
        place_kernel,
        out_shape=jax.ShapeDtypeStruct((2 * BLK, H * DH), jnp.bfloat16),
        in_specs=[pl.BlockSpec(memory_space=pltpu.SMEM)]
        + [pl.BlockSpec(memory_space=pltpu.VMEM)] * 4,
        out_specs=pl.BlockSpec(memory_space=pltpu.VMEM),
    )(starts, *pieces)


def piece_places(blocks, core, y, x):
    dy, dx = (blocks // 8 - y) % 4, (blocks // 2 - x) % 4
    half = blocks // 32 % 2
    small, big = jnp.where(half == 0, dx, dy), jnp.where(half == 0, dy, dx)

    def ring(d):
        return jnp.where(d < 2, 2 * d, 7 - 2 * d)

    inner = blocks // 64 * 4 + blocks % 2
    places = jnp.where(half == core, 0, 512) + ring(big) * 128 + ring(small) * 32 + inner
    return places, jnp.where(big == 0, 0, 1)


def block_lists(place_of, own_blocks, column_blocks, column_count, slash_offsets, slash_count):
    own = jnp.tile(own_blocks, HG)[None, :]
    column = jnp.repeat(column_blocks.T, QB, axis=1)
    column_used = jnp.arange(NV, dtype=jnp.int32)[:, None] < jnp.repeat(column_count, QB)
    slash = own - jnp.repeat(slash_offsets.T, QB, axis=1)
    slash_used = jnp.arange(NS, dtype=jnp.int32)[:, None] < jnp.repeat(slash_count, QB)
    twice = jnp.any((column[None] == slash[:, None]) & column_used[None], axis=1)
    blocks = jnp.concatenate([own, column, jnp.maximum(slash, 0)])
    usable = jnp.concatenate(
        [
            jnp.ones(own.shape, bool),
            column_used & (column < own),
            slash_used & (slash >= 0) & jnp.logical_not(twice),
        ]
    )
    places, parts = place_of(blocks)
    width = 1 + NV + NS
    earlier = (jnp.arange(width)[None, :] < jnp.arange(width)[:, None])[:, :, None]
    slot = jnp.arange(LMAX, dtype=jnp.int32)[:, None, None]
    lists, counts = [], []
    for part in range(PARTS):
        used = usable & (parts == part)
        rank = jnp.sum(used[None] & earlier, axis=1, dtype=jnp.int32)
        live = jnp.sum(used, axis=0, dtype=jnp.int32)
        packed = jnp.where(used[None] & (rank[None] == slot), places[None], 0)
        lists.append(jnp.sum(packed, axis=1))
        counts.append((jnp.max(live.reshape(HG, QB), axis=1) + CB - 1) // CB)
        counts.append(live)
    return jnp.concatenate(lists).reshape(-1), jnp.concatenate(counts)


def device_index(z, core, y, x):
    return ((z * 2 + core) * 4 + y) * 4 + x


def send(array, first, second=None):
    pairs = []
    for z in range(8):
        for y in range(4):
            for x in range(4):
                for core, (dz, dc, dy, dx) in enumerate((first, second or first)):
                    target = ((z + dz) % 8, core ^ dc, (y + dy) % 4, (x + dx) % 4)
                    pairs.append((device_index(z, core, y, x), device_index(*target)))
    return lax.ppermute(array, AXES, pairs)


AXES = ("z", "core", "y", "x")
UP_Y, DOWN_Y, UP_X, DOWN_X = (0, 0, 1, 0), (0, 0, -1, 0), (0, 0, 0, 1), (0, 0, 0, -1)
UP_Z, DOWN_Z, UP_2, DOWN_2 = (1, 0, 0, 0), (-1, 0, 0, 0), (2, 0, 0, 0), (-2, 0, 0, 0)
OTHER = (0, 1, 0, 0)


def gather_and_attend(own, lists, counts, late):
    tie = lax.optimization_barrier
    own, late = tie((own, late))
    up1 = send(own, UP_X, UP_Y)
    down1 = send(own, DOWN_X, DOWN_Y)
    up2 = send(own, (0, 0, 0, 2), (0, 0, 2, 0))
    near_queries = (late[0], send(late[1], UP_Z), send(late[2], DOWN_Z))
    up1, down1, up2, lists, counts, near_queries, far_query = tie(
        (up1, down1, up2, lists, counts, near_queries, late[3])
    )
    queries = near_queries + (send(far_query, UP_2, DOWN_2),)
    near = jnp.concatenate([own, up1, down1, up2])
    a1 = send(near, UP_Y, UP_X)
    b1 = send(near, DOWN_Y, DOWN_X)
    buffer = collect([near], [0], ())
    state = attend(0, lists, counts, queries, buffer, ())
    a1, b1, buffer, state = tie((a1, b1, buffer, state))
    a2 = send(a1[: PIECE // 2], UP_Y, UP_X)
    b2 = send(b1[PIECE // 2 :], DOWN_Y, DOWN_X)
    buffer = collect([a1, b1], [PIECE, 2 * PIECE], buffer)
    a2, b2, buffer = tie((a2, b2, buffer))
    buffer = collect([a2, b2], [3 * PIECE, 3 * PIECE + PIECE // 2], buffer)
    return attend(1, lists, counts, queries, buffer, state)[3:]


def per_device(
    query_rows, key_rows, value_rows, column_blocks, column_count, slash_offsets, slash_count
):
    tokens = query_rows.shape[0]
    z, core, y, x = (lax.axis_index(name) for name in AXES)
    group = z % KVH
    pairs = jnp.stack(
        [array.reshape(tokens, KVH, DH).transpose(1, 0, 2) for array in (key_rows, value_rows)],
        axis=1,
    )
    own = lax.all_to_all(
        jnp.concatenate([pairs, pairs]), "z", split_axis=0, concat_axis=0, tiled=True
    ).reshape(16 * tokens, DH)

    def mine(array):
        return lax.dynamic_slice_in_dim(array, group * HG, HG, 0)

    last = jnp.where(core == 0, z + 6, z + 2)
    sources = jnp.stack([z, z + 7, z + 1, last]) % 8
    own_blocks = ((sources * 2 + core) * 32 + (y * 4 + x) * 2)[:, None] + jnp.arange(2)
    lists, counts = block_lists(
        functools.partial(piece_places, core=core, y=y, x=x),
        own_blocks.reshape(-1).astype(jnp.int32),
        mine(column_blocks),
        mine(column_count),
        mine(slash_offsets),
        mine(slash_count),
    )

    def heads(step):
        start = (z + step) % KVH * (HG * DH)
        return lax.dynamic_slice_in_dim(query_rows, start, HG * DH, 1)

    late = (heads(0), heads(1), heads(3), heads(2))
    outputs = gather_and_attend(own, lists, counts, late)
    pieces = (
        outputs[0],
        send(outputs[1], DOWN_Z),
        send(outputs[2], UP_Z),
        send(outputs[3], DOWN_2, UP_2),
    )
    starts = jnp.stack([z, z + 1, z + 3, z + 2]) % KVH
    return place_heads(starts.astype(jnp.int32), pieces)


def solution(mesh):
    fine = Mesh(mesh.devices.reshape(8, 2, 4, 4), AXES)
    split = P(AXES, None)
    return jax.shard_map(
        per_device,
        mesh=fine,
        in_specs=(split, split, split, P(), P(), P(), P()),
        out_specs=split,
        check_vma=False,
    )
```
